32 devices in a mesh: dp: 16 (over z, y, core), inner: 2 (over x).
Axes of the slice: x: 2, y: 2, z: 4, core: 2. Of those that a mesh axis runs over, the one named last changes fastest.
Arguments:
- tokens: bfloat16 [16384, 1664], P(('dp', 'inner')), may hold values from -16 to 16
- attn_gain: float32 [1664], replicated, may hold values from 0.1 to 1.9
- qkv_weight: bfloat16 [3, 1664, 832], P(None, 'dp', 'inner'), may hold values from -6 to 6
- out_weight: bfloat16 [832, 1664], P('inner', 'dp'), may hold values from -0.21875 to 0.21875
- merge_gain: float32 [6656], replicated, may hold values from 0.25 to 1.75
- merge_weight: bfloat16 [6656, 2048], P('dp', 'inner'), may hold values from -0.078125 to 0.078125
- segment_ids: int32 [16384], P('dp'), may hold values from -1 to 7, as said below
- owners: int32 [4096, 1], P('dp'), may hold values from 0 to 15; in each aligned block of 256 rows (0 to 255, 256 to 511, ...) at most 32 rows name the same one
Outputs:
- merged_out: bfloat16 [8192, 2048], P('dp', 'inner')
The draws below stay inside these ranges and needn't reach their ends.
Inputs may be any that keep to these rules, and one draw needn't show every extreme that they name: `segment_ids`: within each device's aligned block of 512 tokens, ids never fall except to -1, which fills a tail of 4 or more tokens; every run of one id starts at a multiple of 4 and holds a multiple of 4 tokens. `owners`: in each aligned block of 256 rows (the rows of one index of dp) no owner is named by more than 32 rows.
All inputs are finite; a program needn't handle non-finite values.
Results may differ from the reference program's by a relative error of at most 0.0062.
Values may be sent and summed in bfloat16 or wider, within the bound.
A program may use at most 128 MiB of HBM per device.

```python
import math
import jax
import jax.numpy as jnp
import numpy as np
from jax import lax

D = 1664
HEAD_DIM = 104
HEADS = 8
M_OUT = 2048
TOK_DEV = 512
IMG_DEV = 8
HD = 832
MQ_DEV = 128
TOKENS = 16384
MERGED = 4096
GROUP = 256
SLOT = 32
ROWS_OWNER = 512
OUT_ROWS = 8192
N_DP = 16
N_INNER = 2


def draw_tokens(key, part):
    key_rows, key_cols, key_noise = jax.random.split(key, 3)
    row_scale = jnp.exp(jax.random.uniform(key_rows, (TOKENS, 1), jnp.float32, math.log(0.1), 0.0))
    col_scale = jnp.exp(jax.random.uniform(key_cols, (1, D), jnp.float32, math.log(0.3), math.log(3.0)))
    noise = jnp.clip(jax.random.normal(key_noise, (TOKENS, D), jnp.float32), -4.0, 4.0)
    values = noise * col_scale * row_scale
    return values.astype(jnp.bfloat16)


def draw_qkv_weight(key, part):
    key_base = jax.random.fold_in(key, 0)
    base = jnp.clip(jax.random.normal(key_base, (3, D, HEADS, HEAD_DIM), jnp.float32), -4.0, 4.0) * D ** (-0.5)
    return base.reshape(3, D, HEADS * HEAD_DIM).astype(jnp.bfloat16)


def draw_segment_ids(key, part):
    blocks = TOKENS // TOK_DEV
    quads = TOK_DEV // 4
    key_ids, key_pad = jax.random.split(key)
    raw = jax.random.randint(key_ids, (blocks, quads), 0, IMG_DEV)
    ids = jnp.sort(raw, axis=1)
    padding = jax.random.randint(key_pad, (blocks, 1), 1, quads // 4 + 1)
    place = jnp.arange(quads)[None, :]
    live = quads - padding
    ids = jnp.where(place == live - 1, IMG_DEV - 1, ids)
    ids = jnp.where(place >= live, -1, ids)
    return jnp.repeat(ids, 4, axis=1).reshape(TOKENS).astype(jnp.int32)


def block_levels(own_key, dims, shards, smallest, high):
    def one(dim, shards_of):
        steps = jax.random.uniform(jax.random.fold_in(jax.random.fold_in(own_key, 6), dim), (shards_of,), jnp.float32, smallest / len(shards), high / len(shards))
        return jnp.repeat(jnp.exp(steps), dims[dim] // shards_of).reshape((-1,) + (1,) * (len(dims) - dim - 1))

    level = one(*shards[0])
    for cut in shards[1:]:
        level = level * one(*cut)
    return level


def assign_block(own_key, own, number, rows, amount, top, bound, lean):
    sequence = jax.random.permutation(own_key, amount)
    packed, usual = load_shares(amount, rows * top, bound, lean, True), load_shares(amount, rows * top, bound, lean, False)
    places = jnp.arange(amount)

    def named(lengths, rotation):
        used = int((lengths > 0).sum())
        fixed = max(1, used // 4)
        passed = fixed + (places - fixed + rotation * (used - fixed)) % max(1, amount - fixed)
        return jnp.zeros((amount,), jnp.int32).at[sequence[jnp.where(places < fixed, places, passed)]].set(jnp.asarray(lengths, jnp.int32))

    lengths = jnp.where(number % 4 == 0, named(packed, number // 4), named(usual, number - number // 4 - 1))
    mixed = jax.random.permutation(jax.random.fold_in(own, 3), amount)
    source_of, sink = mixed[0:amount // 2 * 2:2], mixed[1:amount // 2 * 2:2]
    slack = jnp.minimum(lengths[source_of] - 1, bound - lengths[sink]) // 2
    slack = jnp.where((source_of == sequence[0]) | (sink == sequence[0]) | (lengths[sink] == 0), 0, jnp.maximum(slack, 0))
    passed = jax.random.randint(jax.random.fold_in(own, 4), (amount // 2,), 0, 1 << 20) % (slack + 1)
    lengths = lengths.at[source_of].add(-passed).at[sink].add(passed)
    members = jnp.searchsorted(jnp.cumsum(lengths), jnp.arange(rows * top), side="right").astype(jnp.int32)
    listing = members.reshape(top, rows).T
    listing = listing[jax.random.permutation(jax.random.fold_in(own, 1), rows)]
    rotation = jax.random.randint(jax.random.fold_in(own, 2), (rows, 1), 0, top)
    return jnp.take_along_axis(listing, (jnp.arange(top)[None, :] + rotation) % top, axis=1)


def load_shares(number_of, total, limit, skew, full):
    weights = [(1 << 20) // math.isqrt(rank ** skew) + 1 for rank in range(1, number_of + 1)]
    largest = limit if full else min(limit, max(-(-total // number_of), total * weights[0] // sum(weights)))
    least = 1 if total - largest >= number_of - 1 else 0
    given, rest = [largest] + [least] * (number_of - 1), total - largest - least * (number_of - 1)
    while rest > 0:
        free = [i for i in range(1, number_of) if given[i] < largest] or [i for i in range(1, number_of) if given[i] < limit]
        mass, remaining = sum([weights[i] for i in free]), rest
        for i in free:
            extra = min(limit - given[i], max(1, remaining * weights[i] // mass), rest)
            given[i] = given[i] + extra
            rest = rest - extra
    return np.array(given)


def scatter_about(rng, shape, scale, bound, cuts=(), kind=jnp.bfloat16):
    drawn = scale * jax.random.normal(rng, shape, jnp.float32)
    if cuts:
        drawn = drawn * block_levels(rng, shape, cuts, -0.22, 0.18)
    return jnp.clip(drawn, -bound, bound).astype(kind)


def setup_inputs(seed: int = 0) -> dict:
    splits = jax.random.split(jax.random.key(seed), 9)
    tokens = draw_tokens(jax.random.fold_in(splits[8], 71), 0)
    attn_gain = jnp.clip(1.0 + 0.18 * jax.random.normal(splits[1], (D,), jnp.float32), 0.1, 1.9)
    qkv_weight = draw_qkv_weight(jax.random.fold_in(splits[8], 71), 0)
    out_weight = scatter_about(splits[3], (HD, D), HD ** -0.5, 0.21875, ((0, 2), (1, 16)))
    merge_gain = jnp.clip(1.0 + 0.15 * jax.random.normal(splits[4], (4 * D,), jnp.float32), 0.25, 1.75)
    merge_weight = scatter_about(splits[5], (4 * D, M_OUT), (4 * D) ** -0.5, 0.078125, ((0, 16), (1, 2)))
    segment_ids = draw_segment_ids(jax.random.fold_in(splits[8], 71), 0)
    owners_keys = jax.random.split(jax.random.fold_in(splits[7], 1), MERGED // GROUP)
    owners_turns = jax.random.permutation(jax.random.fold_in(splits[7], 3), MERGED // GROUP)
    owners = jax.vmap(lambda own, number: assign_block(jax.random.fold_in(splits[7], 2), own, number, GROUP, N_DP, 1, SLOT, 2))(owners_keys, owners_turns).reshape((MERGED, 1))
    return dict(tokens=tokens, attn_gain=attn_gain, qkv_weight=qkv_weight, out_weight=out_weight, merge_gain=merge_gain, merge_weight=merge_weight, segment_ids=segment_ids, owners=owners)


EPS = 1e-06
NEG = -1e+30

def layer_norm(values, gain):
    values = values.astype(jnp.float32)
    center = values - lax.optimization_barrier(jnp.mean(values, axis=-1, keepdims=True))
    spread = lax.optimization_barrier(jnp.mean(center * center, axis=-1, keepdims=True))
    return center * lax.rsqrt(spread + EPS) * gain

def attend(queries, keys, vectors, segment):
    scores = jnp.einsum('qhe,khe->hqk', queries.astype(jnp.float32), keys.astype(jnp.float32)) * HEAD_DIM ** (-0.5)
    visible = segment[:, None] == segment[None, :]
    scores = jnp.where(visible[None, :, :], scores, NEG)
    top = lax.optimization_barrier(jnp.max(scores, axis=-1, keepdims=True))
    weights = jnp.exp(scores - top)
    probs = (weights / lax.optimization_barrier(jnp.sum(weights, axis=-1, keepdims=True))).astype(jnp.bfloat16)
    context = jnp.einsum('hqk,khe->qhe', probs.astype(jnp.float32), vectors.astype(jnp.float32))
    return context.astype(jnp.bfloat16)

def reference(tokens, attn_gain, qkv_weight, out_weight, merge_gain, merge_weight, segment_ids, owners):

    def encode_block(inputs):
        block, segment = inputs
        normed = layer_norm(block, attn_gain).astype(jnp.bfloat16)
        projected = jnp.einsum('td,cdh->cth', normed.astype(jnp.float32), qkv_weight.astype(jnp.float32))
        projected = projected.astype(jnp.bfloat16).reshape(3, TOK_DEV, HEADS, HEAD_DIM)
        context = attend(projected[0], projected[1], projected[2], segment).reshape(TOK_DEV, HD)
        hidden = block.astype(jnp.float32) + jnp.dot(context, out_weight, preferred_element_type=jnp.float32)
        quad_rows = hidden.reshape(MQ_DEV, 4 * D)
        live = segment.reshape(MQ_DEV, 4)[:, 0] >= 0
        merged = jnp.where(live[:, None], layer_norm(quad_rows, merge_gain), 0.0).astype(jnp.bfloat16)
        return jnp.dot(merged, merge_weight, preferred_element_type=jnp.float32).astype(jnp.bfloat16)
    blocks = tokens.reshape(N_DP * N_INNER, TOK_DEV, D)
    segments = segment_ids.reshape(N_DP * N_INNER, TOK_DEV)
    features = lax.map(encode_block, (blocks, segments)).reshape(MERGED, M_OUT)
    owner_col = owners[:, 0].astype(jnp.int32)
    chosen = (owner_col[:, None] == jnp.arange(N_DP, dtype=jnp.int32)[None, :]).astype(jnp.int32)
    chosen = chosen.reshape(N_DP, GROUP, N_DP)
    earlier = jnp.cumsum(chosen, axis=1) - chosen
    rank = lax.optimization_barrier(jnp.sum(earlier * chosen, axis=2)).reshape(MERGED).astype(jnp.int32)
    source = (jnp.arange(MERGED, dtype=jnp.int32) // GROUP).astype(jnp.int32)
    target = owner_col * ROWS_OWNER + source * SLOT + rank
    return jnp.zeros((OUT_ROWS, M_OUT), jnp.bfloat16).at[target].set(features)
```

```python
import functools

import jax
import jax.numpy as jnp
from jax import lax
from jax.experimental import pallas as pl
from jax.experimental.pallas import tpu as pltpu
from jax.sharding import PartitionSpec as P

MESH = pl.DeviceIdType.MESH

HEAD_DIM = 104


EPS = 1e-06
NEG = -1e30


def layer_norm(values, gain):
    values = values.astype(jnp.float32)
    center = values - jnp.mean(values, axis=-1, keepdims=True)
    spread = jnp.mean(center * center, axis=-1, keepdims=True)
    return center * lax.rsqrt(spread + EPS) * gain


def attend_block(queries, keys, vectors, segment):
    scale = queries.shape[-1] ** (-0.5)
    scores = jnp.einsum("qhe,khe->hqk", queries, keys, preferred_element_type=jnp.float32) * scale
    visible = segment[:, None] == segment[None, :]
    scores = jnp.where(visible[None, :, :], scores, NEG)
    top = jnp.max(scores, axis=-1, keepdims=True)
    weights = jnp.exp(scores - top)
    probs = (weights / jnp.sum(weights, axis=-1, keepdims=True)).astype(jnp.bfloat16)
    context = jnp.einsum("hqk,khe->qhe", probs, vectors, preferred_element_type=jnp.float32)
    return context.astype(jnp.bfloat16)


def split_heads(projected):
    shaped = projected.reshape(3, projected.shape[1], projected.shape[2] // HEAD_DIM, HEAD_DIM)
    return (shaped[0], shaped[1], shaped[2])


def local(tokens, attn_gain, qkv_weight, out_weight, merge_gain, merge_weight, segment_ids, owners):
    tok_rows = tokens.shape[0]
    local_segment = lax.dynamic_slice_in_dim(
        segment_ids, lax.axis_index("inner") * tok_rows, tok_rows
    )
    normed = layer_norm(tokens, attn_gain).astype(jnp.bfloat16)
    qkv_part = lax.all_gather(qkv_weight, "inner", axis=2, tiled=True)
    projected = jnp.einsum(
        "td,cdh->cth",
        normed,
        lax.all_gather(qkv_part, "dp", axis=1, tiled=True),
        preferred_element_type=jnp.float32,
    )
    queries, keys, vectors = split_heads(projected.astype(jnp.bfloat16))
    context = attend_block(queries, keys, vectors, local_segment).reshape(tok_rows, -1)
    out_part = lax.all_gather(out_weight, "inner", axis=0, tiled=True)
    attn_out = jnp.dot(
        context,
        lax.all_gather(out_part, "dp", axis=1, tiled=True),
        preferred_element_type=jnp.float32,
    )
    hidden = tokens.astype(jnp.float32) + attn_out
    quad_rows = hidden.reshape(tok_rows // 4, -1)
    live = local_segment.reshape(-1, 4)[:, 0] >= 0
    merged = jnp.where(live[:, None], layer_norm(quad_rows, merge_gain), 0.0).astype(jnp.bfloat16)
    merge_full = lax.all_gather(merge_weight, "dp", axis=0, tiled=True)
    features = jnp.dot(
        lax.all_gather(merged, "inner", axis=0, tiled=True),
        merge_full,
        preferred_element_type=jnp.float32,
    ).astype(jnp.bfloat16)
    n_dp = lax.axis_size("dp")
    group_rows = features.shape[0]
    slots = 2 * group_rows // n_dp
    owner_col = owners[:, 0]
    chosen = (owner_col[:, None] == jnp.arange(n_dp, dtype=jnp.int32)[None, :]).astype(jnp.int32)
    earlier = jnp.cumsum(chosen, axis=0) - chosen
    rank = jnp.sum(earlier * chosen, axis=1)
    target = owner_col * slots + rank
    source_row = (
        jnp.full((n_dp * slots,), group_rows, jnp.int32)
        .at[target]
        .set(jnp.arange(group_rows, dtype=jnp.int32))
    )
    padded = jnp.concatenate([features, jnp.zeros((1, features.shape[1]), jnp.bfloat16)], axis=0)
    outgoing = padded[source_row]
    return lax.all_to_all(outgoing, "dp", split_axis=0, concat_axis=0, tiled=True)


RING = 8


def chip_of(place):
    place = lax.rem(place + 2 * RING, RING)
    row = place // 4
    return 2 * (place + row * (7 - 2 * place)) + row


def gather_kernel(sq, so, gq, go, local_sem, send_sem, recv_sem):
    x = lax.axis_index("inner")
    dp = lax.axis_index("dp")
    core = lax.rem(dp, 2)
    chip = dp // 2
    z, y = chip // 2, lax.rem(chip, 2)
    place = z + y * (7 - 2 * z)
    right = (chip_of(place + 1) * 2 + core, x)
    left = (chip_of(place - 1) * 2 + core, x)
    across = (dp, 1 - x)
    sibling = (chip * 2 + 1 - core, x)
    mine = 2 * x + core
    far = 2 * (1 - x) + core
    split = 112

    barrier = pltpu.get_barrier_semaphore()
    for other in (right, left, across, sibling):
        pl.semaphore_signal(barrier, inc=1, device_id=other, device_id_type=MESH)
    pl.semaphore_wait(barrier, 4)

    pairs = ((sq, gq), (so, go))
    kept = []
    for a, (shard, whole) in enumerate(pairs):
        copy = pltpu.make_async_copy(shard, whole.at[mine, chip], local_sem.at[a])
        copy.start()
        kept.append(copy)

    sent = []

    def block(whole, plane, dist, rows):
        ref = whole.at[plane, chip_of(place + dist)]
        return ref if rows is None else ref.at[pl.ds(*rows)]

    def send(a, slot, plane, dist, device, rows=None):
        whole = pairs[a][1]
        target = block(whole, plane, dist, rows)
        source = pairs[a][0] if plane is mine and dist == 0 else target
        if plane is mine and dist == 0 and rows is not None:
            source = source.at[pl.ds(*rows)]
        copy = pltpu.make_async_remote_copy(
            src_ref=source,
            dst_ref=target,
            send_sem=send_sem.at[a, slot],
            recv_sem=recv_sem.at[a, slot],
            device_id=device,
            device_id_type=MESH,
        )
        copy.start()
        sent.append(copy)

    def arrived(a, slot, plane, dist, device, rows=None):
        target = block(pairs[a][1], plane, dist, rows)
        pltpu.make_async_remote_copy(
            src_ref=target,
            dst_ref=target,
            send_sem=send_sem.at[a, slot],
            recv_sem=recv_sem.at[a, slot],
            device_id=device,
            device_id_type=MESH,
        ).wait_recv()

    def spread(a, dist):
        index = dist % RING
        send(a, 8 + index, mine, dist, across)
        send(a, 16 + index, mine, dist, sibling)

    top, bottom = (0, split), (split, sq.shape[0] - split)
    for a in range(2):
        send(a, 0, mine, 0, right)
        send(a, 4, mine, 0, left)
        spread(a, 0)
    for step in range(1, 4):
        for a in range(2):
            arrived(a, step - 1, mine, -step, left)
            send(a, step, mine, -step, right, top if step == 3 else None)
            spread(a, -step)
            arrived(a, 4 + step - 1, mine, step, right)
            send(a, 4 + step, mine, step, left, bottom if step == 3 else None)
            spread(a, step)
    for a in range(2):
        arrived(a, 3, mine, 4, left, top)
        arrived(a, 7, mine, 4, right, bottom)
        spread(a, 4)
    order = (0, -1, 1, -2, 2, -3, 3, 4)
    for dist in order:
        for a in range(2):
            arrived(a, 8 + dist % RING, far, dist, across)
            send(a, 24 + dist % RING, far, dist, sibling)
    near_other = 2 * x + 1 - core
    far_other = 2 * (1 - x) + 1 - core
    for dist in order:
        for a in range(2):
            arrived(a, 16 + dist % RING, near_other, dist, sibling)
            arrived(a, 24 + dist % RING, far_other, dist, sibling)
    for copy in sent:
        copy.wait_send()
    for copy in kept:
        copy.wait()


def gather_heads(sq, so):
    return pl.pallas_call(
        gather_kernel,
        out_shape=(
            jax.ShapeDtypeStruct((4, RING) + sq.shape, sq.dtype),
            jax.ShapeDtypeStruct((4, RING) + so.shape, so.dtype),
        ),
        in_specs=[pl.BlockSpec(memory_space=pl.ANY)] * 2,
        out_specs=(pl.BlockSpec(memory_space=pl.ANY),) * 2,
        scratch_shapes=[
            pltpu.SemaphoreType.DMA((2,)),
            pltpu.SemaphoreType.DMA((2, 32)),
            pltpu.SemaphoreType.DMA((2, 32)),
        ],
        compiler_params=pltpu.CompilerParams(collective_id=0, has_side_effects=True),
        cost_estimate=pl.CostEstimate(flops=0, bytes_accessed=200_000_000, transcendentals=0),
    )(sq, so)


def pair_shards(qkv_weight, out_weight):
    depth = qkv_weight.shape[1]
    half = qkv_weight.shape[2] // 2
    core = lax.rem(lax.axis_index("dp"), 2)
    heads = qkv_weight.reshape(3, depth, 2, half).transpose(2, 1, 0, 3).reshape(2, depth, 3 * half)
    outs = out_weight.reshape(2, half, depth).transpose(0, 2, 1)
    both = jnp.concatenate([heads, outs], axis=2)
    keep = jnp.where(core == 0, both[0], both[1])
    give = jnp.where(core == 0, both[1], both[0])
    n_dp = lax.axis_size("dp")
    got = lax.ppermute(give, "dp", [(i, i ^ 1) for i in range(n_dp)])
    shard = jnp.concatenate(
        [jnp.where(core == 0, keep, got), jnp.where(core == 0, got, keep)], axis=0
    )
    return shard[:, : 3 * half], shard[:, 3 * half :]


def attend_pairs(projected, segment):
    pairs, rows, width = projected.shape
    shaped = projected.reshape(pairs, rows, 3, 2, HEAD_DIM)
    queries, keys, vectors = shaped[:, :, 0], shaped[:, :, 1], shaped[:, :, 2]
    scale = HEAD_DIM ** (-0.5)
    scores = jnp.einsum("pqhe,pkhe->phqk", queries, keys, preferred_element_type=jnp.float32) * scale
    visible = segment[:, None] == segment[None, :]
    scores = jnp.where(visible[None, None], scores, NEG)
    top = jnp.max(scores, axis=-1, keepdims=True)
    weights = jnp.exp(scores - top)
    probs = (weights / jnp.sum(weights, axis=-1, keepdims=True)).astype(jnp.bfloat16)
    context = jnp.einsum("phqk,pkhe->pqhe", probs, vectors, preferred_element_type=jnp.float32)
    return context.astype(jnp.bfloat16).reshape(pairs, rows, 2 * HEAD_DIM)


def local_ring(tokens, attn_gain, qkv_weight, out_weight, merge_gain, merge_weight, segment_ids, owners):
    tok_rows, width = tokens.shape
    local_segment = lax.dynamic_slice_in_dim(
        segment_ids, lax.axis_index("inner") * tok_rows, tok_rows
    )
    merge_full = lax.all_gather(merge_weight, "dp", axis=0, tiled=True)
    sq, so = pair_shards(qkv_weight, out_weight)
    gq, go = gather_heads(sq, so)
    gq = gq.reshape(4, width, sq.shape[1])
    go = go.reshape(4, width, so.shape[1])
    normed = layer_norm(tokens, attn_gain).astype(jnp.bfloat16)
    projected = jnp.einsum("td,pdn->ptn", normed, gq, preferred_element_type=jnp.float32)
    context = attend_pairs(projected.astype(jnp.bfloat16), local_segment)
    attn_out = jnp.einsum("ptn,pdn->td", context, go, preferred_element_type=jnp.float32)
    hidden = tokens.astype(jnp.float32) + attn_out
    quad_rows = hidden.reshape(tok_rows // 4, -1)
    live = local_segment.reshape(-1, 4)[:, 0] >= 0
    merged = jnp.where(live[:, None], layer_norm(quad_rows, merge_gain), 0.0).astype(jnp.bfloat16)
    theirs = lax.ppermute(merged, "inner", [(0, 1), (1, 0)])
    first = lax.axis_index("inner") == 0
    group = jnp.concatenate(
        [jnp.where(first, merged, theirs), jnp.where(first, theirs, merged)], axis=0
    )
    features = jnp.dot(group, merge_full, preferred_element_type=jnp.float32).astype(jnp.bfloat16)
    n_dp = lax.axis_size("dp")
    group_rows = features.shape[0]
    slots = 2 * group_rows // n_dp
    owner_col = owners[:, 0]
    chosen = (owner_col[:, None] == jnp.arange(n_dp, dtype=jnp.int32)[None, :]).astype(jnp.int32)
    earlier = jnp.cumsum(chosen, axis=0) - chosen
    rank = jnp.sum(earlier * chosen, axis=1)
    target = owner_col * slots + rank
    place = (jnp.arange(n_dp * slots, dtype=jnp.int32)[:, None] == target[None, :]).astype(jnp.bfloat16)
    outgoing = jnp.dot(place, features, preferred_element_type=jnp.float32).astype(jnp.bfloat16)
    return lax.all_to_all(outgoing, "dp", split_axis=0, concat_axis=0, tiled=True)


def solution(mesh):
    placed = (
        P(("dp", "inner"), None),
        P(),
        P(None, "dp", "inner"),
        P("inner", "dp"),
        P(),
        P("dp", "inner"),
        P("dp"),
        P("dp", None),
    )
    ringed = dict(mesh.shape) == {"dp": 16, "inner": 2}
    return jax.shard_map(
        local_ring if ringed else local, mesh=mesh, in_specs=placed, out_specs=P("dp", "inner"), check_vma=False
    )
```

```python
import functools

import jax
import jax.numpy as jnp
from jax import lax
from jax.experimental import pallas as pl
from jax.experimental.pallas import tpu as pltpu
from jax.sharding import PartitionSpec as P

MESH = pl.DeviceIdType.MESH

HEAD_DIM = 104


EPS = 1e-06
NEG = -1e30


def layer_norm(values, gain):
    values = values.astype(jnp.float32)
    center = values - jnp.mean(values, axis=-1, keepdims=True)
    spread = jnp.mean(center * center, axis=-1, keepdims=True)
    return center * lax.rsqrt(spread + EPS) * gain


def attend_block(queries, keys, vectors, segment):
    scale = queries.shape[-1] ** (-0.5)
    scores = jnp.einsum("qhe,khe->hqk", queries, keys, preferred_element_type=jnp.float32) * scale
    visible = segment[:, None] == segment[None, :]
    scores = jnp.where(visible[None, :, :], scores, NEG)
    top = jnp.max(scores, axis=-1, keepdims=True)
    weights = jnp.exp(scores - top)
    probs = (weights / jnp.sum(weights, axis=-1, keepdims=True)).astype(jnp.bfloat16)
    context = jnp.einsum("hqk,khe->qhe", probs, vectors, preferred_element_type=jnp.float32)
    return context.astype(jnp.bfloat16)


def split_heads(projected):
    shaped = projected.reshape(3, projected.shape[1], projected.shape[2] // HEAD_DIM, HEAD_DIM)
    return (shaped[0], shaped[1], shaped[2])


def local(tokens, attn_gain, qkv_weight, out_weight, merge_gain, merge_weight, segment_ids, owners):
    tok_rows = tokens.shape[0]
    local_segment = lax.dynamic_slice_in_dim(
        segment_ids, lax.axis_index("inner") * tok_rows, tok_rows
    )
    normed = layer_norm(tokens, attn_gain).astype(jnp.bfloat16)
    qkv_part = lax.all_gather(qkv_weight, "inner", axis=2, tiled=True)
    projected = jnp.einsum(
        "td,cdh->cth",
        normed,
        lax.all_gather(qkv_part, "dp", axis=1, tiled=True),
        preferred_element_type=jnp.float32,
    )
    queries, keys, vectors = split_heads(projected.astype(jnp.bfloat16))
    context = attend_block(queries, keys, vectors, local_segment).reshape(tok_rows, -1)
    out_part = lax.all_gather(out_weight, "inner", axis=0, tiled=True)
    attn_out = jnp.dot(
        context,
        lax.all_gather(out_part, "dp", axis=1, tiled=True),
        preferred_element_type=jnp.float32,
    )
    hidden = tokens.astype(jnp.float32) + attn_out
    quad_rows = hidden.reshape(tok_rows // 4, -1)
    live = local_segment.reshape(-1, 4)[:, 0] >= 0
    merged = jnp.where(live[:, None], layer_norm(quad_rows, merge_gain), 0.0).astype(jnp.bfloat16)
    merge_full = lax.all_gather(merge_weight, "dp", axis=0, tiled=True)
    features = jnp.dot(
        lax.all_gather(merged, "inner", axis=0, tiled=True),
        merge_full,
        preferred_element_type=jnp.float32,
    ).astype(jnp.bfloat16)
    n_dp = lax.axis_size("dp")
    group_rows = features.shape[0]
    slots = 2 * group_rows // n_dp
    owner_col = owners[:, 0]
    chosen = (owner_col[:, None] == jnp.arange(n_dp, dtype=jnp.int32)[None, :]).astype(jnp.int32)
    earlier = jnp.cumsum(chosen, axis=0) - chosen
    rank = jnp.sum(earlier * chosen, axis=1)
    target = owner_col * slots + rank
    source_row = (
        jnp.full((n_dp * slots,), group_rows, jnp.int32)
        .at[target]
        .set(jnp.arange(group_rows, dtype=jnp.int32))
    )
    padded = jnp.concatenate([features, jnp.zeros((1, features.shape[1]), jnp.bfloat16)], axis=0)
    outgoing = padded[source_row]
    return lax.all_to_all(outgoing, "dp", split_axis=0, concat_axis=0, tiled=True)


RING = 8


def chip_of(place):
    place = lax.rem(place + 2 * RING, RING)
    row = place // 4
    return 2 * (place + row * (7 - 2 * place)) + row


def gather_kernel(sq, so, gq, go, local_sem, send_sem, recv_sem):
    x = lax.axis_index("inner")
    dp = lax.axis_index("dp")
    core = lax.rem(dp, 2)
    chip = dp // 2
    z, y = chip // 2, lax.rem(chip, 2)
    place = z + y * (7 - 2 * z)
    right = (chip_of(place + 1) * 2 + core, x)
    left = (chip_of(place - 1) * 2 + core, x)
    across = (dp, 1 - x)
    sibling = (chip * 2 + 1 - core, x)
    mine = 2 * x + core
    far = 2 * (1 - x) + core
    split = 112

    barrier = pltpu.get_barrier_semaphore()
    for other in (right, left, across, sibling):
        pl.semaphore_signal(barrier, inc=1, device_id=other, device_id_type=MESH)
    pl.semaphore_wait(barrier, 4)

    pairs = ((sq, gq), (so, go))
    kept = []
    for a, (shard, whole) in enumerate(pairs):
        copy = pltpu.make_async_copy(shard, whole.at[mine, chip], local_sem.at[a])
        copy.start()
        kept.append(copy)

    sent = []

    def block(whole, plane, dist, rows):
        ref = whole.at[plane, chip_of(place + dist)]
        return ref if rows is None else ref.at[pl.ds(*rows)]

    def send(a, slot, plane, dist, device, rows=None):
        whole = pairs[a][1]
        target = block(whole, plane, dist, rows)
        source = pairs[a][0] if plane is mine and dist == 0 else target
        if plane is mine and dist == 0 and rows is not None:
            source = source.at[pl.ds(*rows)]
        copy = pltpu.make_async_remote_copy(
            src_ref=source,
            dst_ref=target,
            send_sem=send_sem.at[a, slot],
            recv_sem=recv_sem.at[a, slot],
            device_id=device,
            device_id_type=MESH,
        )
        copy.start()
        sent.append(copy)

    def arrived(a, slot, plane, dist, device, rows=None):
        target = block(pairs[a][1], plane, dist, rows)
        pltpu.make_async_remote_copy(
            src_ref=target,
            dst_ref=target,
            send_sem=send_sem.at[a, slot],
            recv_sem=recv_sem.at[a, slot],
            device_id=device,
            device_id_type=MESH,
        ).wait_recv()

    def spread(a, dist):
        index = dist % RING
        send(a, 8 + index, mine, dist, across)
        send(a, 16 + index, mine, dist, sibling)

    top, bottom = (0, split), (split, sq.shape[0] - split)
    for a in range(2):
        send(a, 0, mine, 0, right)
        send(a, 4, mine, 0, left)
        spread(a, 0)
    for step in range(1, 4):
        for a in range(2):
            arrived(a, step - 1, mine, -step, left)
            send(a, step, mine, -step, right, top if step == 3 else None)
            spread(a, -step)
            arrived(a, 4 + step - 1, mine, step, right)
            send(a, 4 + step, mine, step, left, bottom if step == 3 else None)
            spread(a, step)
    for a in range(2):
        arrived(a, 3, mine, 4, left, top)
        arrived(a, 7, mine, 4, right, bottom)
        spread(a, 4)
    order = (0, -1, 1, -2, 2, -3, 3, 4)
    for dist in order:
        for a in range(2):
            arrived(a, 8 + dist % RING, far, dist, across)
            send(a, 24 + dist % RING, far, dist, sibling)
    near_other = 2 * x + 1 - core
    far_other = 2 * (1 - x) + 1 - core
    for dist in order:
        for a in range(2):
            arrived(a, 16 + dist % RING, near_other, dist, sibling)
            arrived(a, 24 + dist % RING, far_other, dist, sibling)
    for copy in sent:
        copy.wait_send()
    for copy in kept:
        copy.wait()


def gather_heads(sq, so):
    return pl.pallas_call(
        gather_kernel,
        out_shape=(
            jax.ShapeDtypeStruct((4, RING) + sq.shape, sq.dtype),
            jax.ShapeDtypeStruct((4, RING) + so.shape, so.dtype),
        ),
        in_specs=[pl.BlockSpec(memory_space=pl.ANY)] * 2,
        out_specs=(pl.BlockSpec(memory_space=pl.ANY),) * 2,
        scratch_shapes=[
            pltpu.SemaphoreType.DMA((2,)),
            pltpu.SemaphoreType.DMA((2, 32)),
            pltpu.SemaphoreType.DMA((2, 32)),
        ],
        compiler_params=pltpu.CompilerParams(collective_id=0, has_side_effects=True),
        cost_estimate=pl.CostEstimate(flops=0, bytes_accessed=200_000_000, transcendentals=0),
    )(sq, so)


TAIL_COLS = 256


def tail_kernel(own, theirs, weight, place, out, rows, wide, feat, load_sem, keep_sem, send_sem, recv_sem):
    x = lax.axis_index("inner")
    me = lax.axis_index("dp")
    peers = lax.axis_size("dp")
    half = own.shape[0]
    slots = out.shape[0] // peers
    chunks = weight.shape[1] // TAIL_COLS

    loads = [
        pltpu.make_async_copy(own, rows.at[pl.ds(0, half)], load_sem.at[chunks]),
        pltpu.make_async_copy(theirs, rows.at[pl.ds(half, half)], load_sem.at[chunks + 1]),
    ]
    for chunk in range(chunks):
        loads.append(
            pltpu.make_async_copy(
                weight.at[:, pl.ds(chunk * TAIL_COLS, TAIL_COLS)], wide.at[chunk], load_sem.at[chunk]
            )
        )
    for load in loads:
        load.start()

    barrier = pltpu.get_barrier_semaphore()
    for step in range(1, peers):
        other = lax.rem(me + step, peers)
        pl.semaphore_signal(barrier, inc=1, device_id=(other, x), device_id_type=MESH)
    loads[0].wait()
    loads[1].wait()

    copies = []
    for chunk in range(chunks):
        loads[2 + chunk].wait()
        product = jnp.dot(rows[...], wide[chunk], preferred_element_type=jnp.float32)
        feat[chunk] = jnp.dot(
            place[...], product.astype(jnp.bfloat16), preferred_element_type=jnp.float32
        ).astype(jnp.bfloat16)
        if chunk == 0:
            pl.semaphore_wait(barrier, peers - 1)
        columns = pl.ds(chunk * TAIL_COLS, TAIL_COLS)
        landing = out.at[pl.ds(pl.multiple_of(me * slots, slots), slots), columns]
        for step in range(1, peers):
            other = lax.rem(me + step, peers)
            copy = pltpu.make_async_remote_copy(
                src_ref=feat.at[chunk, pl.ds(pl.multiple_of(other * slots, slots), slots)],
                dst_ref=landing,
                send_sem=send_sem.at[chunk, step],
                recv_sem=recv_sem.at[chunk, step],
                device_id=(other, x),
                device_id_type=MESH,
            )
            copy.start()
            copies.append(copy)
        keep = pltpu.make_async_copy(
            feat.at[chunk, pl.ds(pl.multiple_of(me * slots, slots), slots)], landing, keep_sem.at[chunk]
        )
        keep.start()
        copies.append(keep)
    for chunk in range(chunks):
        columns = pl.ds(chunk * TAIL_COLS, TAIL_COLS)
        for step in range(1, peers):
            giver = lax.rem(me + peers - step, peers)
            landing = out.at[pl.ds(pl.multiple_of(giver * slots, slots), slots), columns]
            pltpu.make_async_remote_copy(
                src_ref=landing,
                dst_ref=landing,
                send_sem=send_sem.at[chunk, step],
                recv_sem=recv_sem.at[chunk, step],
                device_id=(giver, x),
                device_id_type=MESH,
            ).wait_recv()
    for number, copy in enumerate(copies):
        if number % peers == peers - 1:
            copy.wait()
        else:
            copy.wait_send()


def merge_and_route(own, theirs, weight, place):
    peers = lax.axis_size("dp")
    out_rows, group = place.shape
    depth, columns = weight.shape
    chunks = columns // TAIL_COLS
    return pl.pallas_call(
        tail_kernel,
        out_shape=jax.ShapeDtypeStruct((out_rows, columns), jnp.bfloat16),
        in_specs=[pl.BlockSpec(memory_space=pl.ANY)] * 3 + [pl.BlockSpec(memory_space=pltpu.VMEM)],
        out_specs=pl.BlockSpec(memory_space=pl.ANY),
        scratch_shapes=[
            pltpu.VMEM((group, depth), jnp.bfloat16),
            pltpu.VMEM((chunks, depth, TAIL_COLS), jnp.bfloat16),
            pltpu.VMEM((chunks, out_rows, TAIL_COLS), jnp.bfloat16),
            pltpu.SemaphoreType.DMA((chunks + 2,)),
            pltpu.SemaphoreType.DMA((chunks,)),
            pltpu.SemaphoreType.DMA((chunks, peers)),
            pltpu.SemaphoreType.DMA((chunks, peers)),
        ],
        compiler_params=pltpu.CompilerParams(
            collective_id=1, has_side_effects=True, vmem_limit_bytes=56 * 1024 * 1024
        ),
        cost_estimate=pl.CostEstimate(
            flops=2 * group * depth * columns, bytes_accessed=2 * depth * columns, transcendentals=0
        ),
    )(own, theirs, weight, place)


def pair_shards(qkv_weight, out_weight):
    depth = qkv_weight.shape[1]
    half = qkv_weight.shape[2] // 2
    core = lax.rem(lax.axis_index("dp"), 2)
    heads = qkv_weight.reshape(3, depth, 2, half).transpose(2, 1, 0, 3).reshape(2, depth, 3 * half)
    outs = out_weight.reshape(2, half, depth).transpose(0, 2, 1)
    both = jnp.concatenate([heads, outs], axis=2)
    keep = jnp.where(core == 0, both[0], both[1])
    give = jnp.where(core == 0, both[1], both[0])
    n_dp = lax.axis_size("dp")
    got = lax.ppermute(give, "dp", [(i, i ^ 1) for i in range(n_dp)])
    shard = jnp.concatenate(
        [jnp.where(core == 0, keep, got), jnp.where(core == 0, got, keep)], axis=0
    )
    return shard[:, : 3 * half], shard[:, 3 * half :]


def attend_pairs(projected, segment):
    pairs, rows, width = projected.shape
    shaped = projected.reshape(pairs, rows, 3, 2, HEAD_DIM)
    queries, keys, vectors = shaped[:, :, 0], shaped[:, :, 1], shaped[:, :, 2]
    scale = HEAD_DIM ** (-0.5)
    scores = jnp.einsum("pqhe,pkhe->phqk", queries, keys, preferred_element_type=jnp.float32) * scale
    visible = segment[:, None] == segment[None, :]
    scores = jnp.where(visible[None, None], scores, NEG)
    top = jnp.max(scores, axis=-1, keepdims=True)
    weights = jnp.exp(scores - top)
    probs = (weights / jnp.sum(weights, axis=-1, keepdims=True)).astype(jnp.bfloat16)
    context = jnp.einsum("phqk,pkhe->pqhe", probs, vectors, preferred_element_type=jnp.float32)
    return context.astype(jnp.bfloat16).reshape(pairs, rows, 2 * HEAD_DIM)


def local_ring(tokens, attn_gain, qkv_weight, out_weight, merge_gain, merge_weight, segment_ids, owners):
    tok_rows, width = tokens.shape
    local_segment = lax.dynamic_slice_in_dim(
        segment_ids, lax.axis_index("inner") * tok_rows, tok_rows
    )
    merge_full = lax.all_gather(merge_weight, "dp", axis=0, tiled=True)
    sq, so = pair_shards(qkv_weight, out_weight)
    gq, go = gather_heads(sq, so)
    gq = gq.reshape(4, width, sq.shape[1])
    go = go.reshape(4, width, so.shape[1])
    normed = layer_norm(tokens, attn_gain).astype(jnp.bfloat16)
    projected = jnp.einsum("td,pdn->ptn", normed, gq, preferred_element_type=jnp.float32)
    context = attend_pairs(projected.astype(jnp.bfloat16), local_segment)
    attn_out = jnp.einsum("ptn,pdn->td", context, go, preferred_element_type=jnp.float32)
    hidden = tokens.astype(jnp.float32) + attn_out
    quad_rows = hidden.reshape(tok_rows // 4, -1)
    live = local_segment.reshape(-1, 4)[:, 0] >= 0
    merged = jnp.where(live[:, None], layer_norm(quad_rows, merge_gain), 0.0).astype(jnp.bfloat16)
    theirs = lax.ppermute(merged, "inner", [(0, 1), (1, 0)])
    n_dp = lax.axis_size("dp")
    half_rows = merged.shape[0]
    slots = 4 * half_rows // n_dp
    owner_col = owners[:, 0]
    chosen = (owner_col[:, None] == jnp.arange(n_dp, dtype=jnp.int32)[None, :]).astype(jnp.int32)
    earlier = jnp.cumsum(chosen, axis=0) - chosen
    rank = jnp.sum(earlier * chosen, axis=1)
    target = owner_col * slots + rank
    target = jnp.where(
        lax.axis_index("inner") == 0,
        target,
        jnp.concatenate([target[half_rows:], target[:half_rows]]),
    )
    place = (jnp.arange(n_dp * slots, dtype=jnp.int32)[:, None] == target[None, :]).astype(jnp.bfloat16)
    return merge_and_route(merged, theirs, merge_full, place)


def solution(mesh):
    placed = (
        P(("dp", "inner"), None),
        P(),
        P(None, "dp", "inner"),
        P("inner", "dp"),
        P(),
        P("dp", "inner"),
        P("dp"),
        P("dp", None),
    )
    ringed = dict(mesh.shape) == {"dp": 16, "inner": 2}
    return jax.shard_map(
        local_ring if ringed else local, mesh=mesh, in_specs=placed, out_specs=P("dp", "inner"), check_vma=False
    )
```

```python
import functools

import jax
import jax.numpy as jnp
from jax import lax
from jax.experimental import pallas as pl
from jax.experimental.pallas import tpu as pltpu
from jax.sharding import PartitionSpec as P

MESH = pl.DeviceIdType.MESH

HEAD_DIM = 104


EPS = 1e-06
NEG = -1e30


def layer_norm(values, gain):
    values = values.astype(jnp.float32)
    center = values - jnp.mean(values, axis=-1, keepdims=True)
    spread = jnp.mean(center * center, axis=-1, keepdims=True)
    return center * lax.rsqrt(spread + EPS) * gain


def attend_block(queries, keys, vectors, segment):
    scale = queries.shape[-1] ** (-0.5)
    scores = jnp.einsum("qhe,khe->hqk", queries, keys, preferred_element_type=jnp.float32) * scale
    visible = segment[:, None] == segment[None, :]
    scores = jnp.where(visible[None, :, :], scores, NEG)
    top = jnp.max(scores, axis=-1, keepdims=True)
    weights = jnp.exp(scores - top)
    probs = (weights / jnp.sum(weights, axis=-1, keepdims=True)).astype(jnp.bfloat16)
    context = jnp.einsum("hqk,khe->qhe", probs, vectors, preferred_element_type=jnp.float32)
    return context.astype(jnp.bfloat16)


def split_heads(projected):
    shaped = projected.reshape(3, projected.shape[1], projected.shape[2] // HEAD_DIM, HEAD_DIM)
    return (shaped[0], shaped[1], shaped[2])


def local(tokens, attn_gain, qkv_weight, out_weight, merge_gain, merge_weight, segment_ids, owners):
    tok_rows = tokens.shape[0]
    local_segment = lax.dynamic_slice_in_dim(
        segment_ids, lax.axis_index("inner") * tok_rows, tok_rows
    )
    normed = layer_norm(tokens, attn_gain).astype(jnp.bfloat16)
    qkv_part = lax.all_gather(qkv_weight, "inner", axis=2, tiled=True)
    projected = jnp.einsum(
        "td,cdh->cth",
        normed,
        lax.all_gather(qkv_part, "dp", axis=1, tiled=True),
        preferred_element_type=jnp.float32,
    )
    queries, keys, vectors = split_heads(projected.astype(jnp.bfloat16))
    context = attend_block(queries, keys, vectors, local_segment).reshape(tok_rows, -1)
    out_part = lax.all_gather(out_weight, "inner", axis=0, tiled=True)
    attn_out = jnp.dot(
        context,
        lax.all_gather(out_part, "dp", axis=1, tiled=True),
        preferred_element_type=jnp.float32,
    )
    hidden = tokens.astype(jnp.float32) + attn_out
    quad_rows = hidden.reshape(tok_rows // 4, -1)
    live = local_segment.reshape(-1, 4)[:, 0] >= 0
    merged = jnp.where(live[:, None], layer_norm(quad_rows, merge_gain), 0.0).astype(jnp.bfloat16)
    merge_full = lax.all_gather(merge_weight, "dp", axis=0, tiled=True)
    features = jnp.dot(
        lax.all_gather(merged, "inner", axis=0, tiled=True),
        merge_full,
        preferred_element_type=jnp.float32,
    ).astype(jnp.bfloat16)
    n_dp = lax.axis_size("dp")
    group_rows = features.shape[0]
    slots = 2 * group_rows // n_dp
    owner_col = owners[:, 0]
    chosen = (owner_col[:, None] == jnp.arange(n_dp, dtype=jnp.int32)[None, :]).astype(jnp.int32)
    earlier = jnp.cumsum(chosen, axis=0) - chosen
    rank = jnp.sum(earlier * chosen, axis=1)
    target = owner_col * slots + rank
    source_row = (
        jnp.full((n_dp * slots,), group_rows, jnp.int32)
        .at[target]
        .set(jnp.arange(group_rows, dtype=jnp.int32))
    )
    padded = jnp.concatenate([features, jnp.zeros((1, features.shape[1]), jnp.bfloat16)], axis=0)
    outgoing = padded[source_row]
    return lax.all_to_all(outgoing, "dp", split_axis=0, concat_axis=0, tiled=True)


RING = 8


def chip_of(place):
    place = lax.rem(place + 2 * RING, RING)
    row = place // 4
    return 2 * (place + row * (7 - 2 * place)) + row


def gather_kernel(sq, so, gq, go, local_sem, send_sem, recv_sem):
    x = lax.axis_index("inner")
    dp = lax.axis_index("dp")
    core = lax.rem(dp, 2)
    chip = dp // 2
    z, y = chip // 2, lax.rem(chip, 2)
    place = z + y * (7 - 2 * z)
    right = (chip_of(place + 1) * 2 + core, x)
    left = (chip_of(place - 1) * 2 + core, x)
    across = (dp, 1 - x)
    sibling = (chip * 2 + 1 - core, x)
    mine = 2 * x + core
    far = 2 * (1 - x) + core
    split = 112

    barrier = pltpu.get_barrier_semaphore()
    for other in (right, left, across, sibling):
        pl.semaphore_signal(barrier, inc=1, device_id=other, device_id_type=MESH)
    pl.semaphore_wait(barrier, 4)

    pairs = ((sq, gq), (so, go))
    kept = []
    for a, (shard, whole) in enumerate(pairs):
        copy = pltpu.make_async_copy(shard, whole.at[mine, chip], local_sem.at[a])
        copy.start()
        kept.append(copy)

    sent = []

    def block(whole, plane, dist, rows):
        ref = whole.at[plane, chip_of(place + dist)]
        return ref if rows is None else ref.at[pl.ds(*rows)]

    def send(a, slot, plane, dist, device, rows=None):
        whole = pairs[a][1]
        target = block(whole, plane, dist, rows)
        source = pairs[a][0] if plane is mine and dist == 0 else target
        if plane is mine and dist == 0 and rows is not None:
            source = source.at[pl.ds(*rows)]
        copy = pltpu.make_async_remote_copy(
            src_ref=source,
            dst_ref=target,
            send_sem=send_sem.at[a, slot],
            recv_sem=recv_sem.at[a, slot],
            device_id=device,
            device_id_type=MESH,
        )
        copy.start()
        sent.append(copy)

    def arrived(a, slot, plane, dist, device, rows=None):
        target = block(pairs[a][1], plane, dist, rows)
        pltpu.make_async_remote_copy(
            src_ref=target,
            dst_ref=target,
            send_sem=send_sem.at[a, slot],
            recv_sem=recv_sem.at[a, slot],
            device_id=device,
            device_id_type=MESH,
        ).wait_recv()

    def spread(a, dist):
        index = dist % RING
        send(a, 8 + index, mine, dist, across)
        send(a, 16 + index, mine, dist, sibling)

    top, bottom = (0, split), (split, sq.shape[0] - split)
    for a in range(2):
        send(a, 0, mine, 0, right)
        send(a, 4, mine, 0, left)
        spread(a, 0)
    for step in range(1, 4):
        for a in range(2):
            arrived(a, step - 1, mine, -step, left)
            send(a, step, mine, -step, right, top if step == 3 else None)
            spread(a, -step)
            arrived(a, 4 + step - 1, mine, step, right)
            send(a, 4 + step, mine, step, left, bottom if step == 3 else None)
            spread(a, step)
    for a in range(2):
        arrived(a, 3, mine, 4, left, top)
        arrived(a, 7, mine, 4, right, bottom)
        spread(a, 4)
    order = (0, -1, 1, -2, 2, -3, 3, 4)
    for dist in order:
        for a in range(2):
            arrived(a, 8 + dist % RING, far, dist, across)
            send(a, 24 + dist % RING, far, dist, sibling)
    near_other = 2 * x + 1 - core
    far_other = 2 * (1 - x) + 1 - core
    for dist in order:
        for a in range(2):
            arrived(a, 16 + dist % RING, near_other, dist, sibling)
            arrived(a, 24 + dist % RING, far_other, dist, sibling)
    for copy in sent:
        copy.wait_send()
    for copy in kept:
        copy.wait()


def gather_heads(sq, so):
    return pl.pallas_call(
        gather_kernel,
        out_shape=(
            jax.ShapeDtypeStruct((4, RING) + sq.shape, sq.dtype),
            jax.ShapeDtypeStruct((4, RING) + so.shape, so.dtype),
        ),
        in_specs=[pl.BlockSpec(memory_space=pl.ANY)] * 2,
        out_specs=(pl.BlockSpec(memory_space=pl.ANY),) * 2,
        scratch_shapes=[
            pltpu.SemaphoreType.DMA((2,)),
            pltpu.SemaphoreType.DMA((2, 32)),
            pltpu.SemaphoreType.DMA((2, 32)),
        ],
        compiler_params=pltpu.CompilerParams(collective_id=0, has_side_effects=True),
        cost_estimate=pl.CostEstimate(flops=0, bytes_accessed=200_000_000, transcendentals=0),
    )(sq, so)


TAIL_COLS = 256


def tail_kernel(parts, *refs):
    merge_parts(refs[:parts], *refs[parts:])


def merge_parts(pieces, weight, place, out, rows, wide, feat, load_sem, keep_sem, send_sem, recv_sem):
    x = lax.axis_index("inner")
    me = lax.axis_index("dp")
    peers = lax.axis_size("dp")
    piece = pieces[0].shape[0]
    slots = out.shape[0] // peers
    chunks = weight.shape[1] // TAIL_COLS

    loads = [
        pltpu.make_async_copy(ref, rows.at[pl.ds(number * piece, piece)], load_sem.at[chunks + number])
        for number, ref in enumerate(pieces)
    ]
    for chunk in range(chunks):
        loads.append(
            pltpu.make_async_copy(
                weight.at[:, pl.ds(chunk * TAIL_COLS, TAIL_COLS)], wide.at[chunk], load_sem.at[chunk]
            )
        )
    for load in loads:
        load.start()

    barrier = pltpu.get_barrier_semaphore()
    for step in range(1, peers):
        other = lax.rem(me + step, peers)
        pl.semaphore_signal(barrier, inc=1, device_id=(other, x), device_id_type=MESH)
    for number in range(len(pieces)):
        loads[number].wait()

    copies = []
    for chunk in range(chunks):
        loads[len(pieces) + chunk].wait()
        product = jnp.dot(rows[...], wide[chunk], preferred_element_type=jnp.float32)
        feat[chunk] = jnp.dot(
            place[...], product.astype(jnp.bfloat16), preferred_element_type=jnp.float32
        ).astype(jnp.bfloat16)
        if chunk == 0:
            pl.semaphore_wait(barrier, peers - 1)
        columns = pl.ds(chunk * TAIL_COLS, TAIL_COLS)
        landing = out.at[pl.ds(pl.multiple_of(me * slots, slots), slots), columns]
        for step in range(1, peers):
            other = lax.rem(me + step, peers)
            copy = pltpu.make_async_remote_copy(
                src_ref=feat.at[chunk, pl.ds(pl.multiple_of(other * slots, slots), slots)],
                dst_ref=landing,
                send_sem=send_sem.at[chunk, step],
                recv_sem=recv_sem.at[chunk, step],
                device_id=(other, x),
                device_id_type=MESH,
            )
            copy.start()
            copies.append(copy)
        keep = pltpu.make_async_copy(
            feat.at[chunk, pl.ds(pl.multiple_of(me * slots, slots), slots)], landing, keep_sem.at[chunk]
        )
        keep.start()
        copies.append(keep)
    for chunk in range(chunks):
        columns = pl.ds(chunk * TAIL_COLS, TAIL_COLS)
        for step in range(1, peers):
            giver = lax.rem(me + peers - step, peers)
            landing = out.at[pl.ds(pl.multiple_of(giver * slots, slots), slots), columns]
            pltpu.make_async_remote_copy(
                src_ref=landing,
                dst_ref=landing,
                send_sem=send_sem.at[chunk, step],
                recv_sem=recv_sem.at[chunk, step],
                device_id=(giver, x),
                device_id_type=MESH,
            ).wait_recv()
    for number, copy in enumerate(copies):
        if number % peers == peers - 1:
            copy.wait()
        else:
            copy.wait_send()


def merge_and_route(pieces, weight, place, collective_id):
    peers = lax.axis_size("dp")
    out_rows, group = place.shape
    depth, columns = weight.shape
    chunks = columns // TAIL_COLS
    return pl.pallas_call(
        functools.partial(tail_kernel, len(pieces)),
        out_shape=jax.ShapeDtypeStruct((out_rows, columns), jnp.bfloat16),
        in_specs=[pl.BlockSpec(memory_space=pltpu.VMEM)] * len(pieces)
        + [pl.BlockSpec(memory_space=pl.ANY), pl.BlockSpec(memory_space=pltpu.VMEM)],
        out_specs=pl.BlockSpec(memory_space=pltpu.VMEM),
        scratch_shapes=[
            pltpu.VMEM((group, depth), jnp.bfloat16),
            pltpu.VMEM((chunks, depth, TAIL_COLS), jnp.bfloat16),
            pltpu.VMEM((chunks, out_rows, TAIL_COLS), jnp.bfloat16),
            pltpu.SemaphoreType.DMA((chunks + len(pieces),)),
            pltpu.SemaphoreType.DMA((chunks,)),
            pltpu.SemaphoreType.DMA((chunks, peers)),
            pltpu.SemaphoreType.DMA((chunks, peers)),
        ],
        compiler_params=pltpu.CompilerParams(
            collective_id=collective_id, has_side_effects=True, vmem_limit_bytes=56 * 1024 * 1024
        ),
        cost_estimate=pl.CostEstimate(
            flops=2 * group * depth * columns, bytes_accessed=2 * depth * columns, transcendentals=0
        ),
    )(*pieces, weight, place)


def pair_shards(qkv_weight, out_weight):
    depth = qkv_weight.shape[1]
    half = qkv_weight.shape[2] // 2
    core = lax.rem(lax.axis_index("dp"), 2)
    heads = qkv_weight.reshape(3, depth, 2, half).transpose(2, 1, 0, 3).reshape(2, depth, 3 * half)
    outs = out_weight.reshape(2, half, depth).transpose(0, 2, 1)
    both = jnp.concatenate([heads, outs], axis=2)
    keep = jnp.where(core == 0, both[0], both[1])
    give = jnp.where(core == 0, both[1], both[0])
    n_dp = lax.axis_size("dp")
    got = lax.ppermute(give, "dp", [(i, i ^ 1) for i in range(n_dp)])
    shard = jnp.concatenate(
        [jnp.where(core == 0, keep, got), jnp.where(core == 0, got, keep)], axis=0
    )
    return shard[:, : 3 * half], shard[:, 3 * half :]


def attend_pairs(queries, keys, vectors, own_segment, segment):
    pairs, rows = queries.shape[:2]
    scale = HEAD_DIM ** (-0.5)
    scores = jnp.einsum("pqhe,pkhe->phqk", queries, keys, preferred_element_type=jnp.float32) * scale
    visible = own_segment[:, None] == segment[None, :]
    scores = jnp.where(visible[None, None], scores, NEG)
    top = jnp.max(scores, axis=-1, keepdims=True)
    weights = jnp.exp(scores - top)
    probs = (weights / jnp.sum(weights, axis=-1, keepdims=True)).astype(jnp.bfloat16)
    context = jnp.einsum("phqk,pkhe->pqhe", probs, vectors, preferred_element_type=jnp.float32)
    return context.astype(jnp.bfloat16).reshape(pairs, rows, 2 * HEAD_DIM)


def local_ring(tokens, attn_gain, qkv_weight, out_weight, merge_gain, merge_weight, segment_ids, owners):
    tok_rows, width = tokens.shape
    local_segment = lax.dynamic_slice_in_dim(
        segment_ids, lax.axis_index("inner") * tok_rows, tok_rows
    )
    cut = merge_weight.shape[1] // 2
    merge_halves = [
        lax.all_gather(merge_weight[:, part * cut : (part + 1) * cut], "dp", axis=0, tiled=True)
        for part in range(2)
    ]
    sq, so = pair_shards(qkv_weight, out_weight)
    gq, go = gather_heads(sq, so)
    gq = gq.reshape(4, width, sq.shape[1])
    go = go.reshape(4, width, so.shape[1])
    normed = layer_norm(tokens, attn_gain).astype(jnp.bfloat16)
    projected = jnp.einsum("td,pdn->ptn", normed, gq, preferred_element_type=jnp.float32)
    shaped = projected.astype(jnp.bfloat16).reshape(4, tok_rows, 3, 2, HEAD_DIM)
    queries, keys, vectors = shaped[:, :, 0], shaped[:, :, 1], shaped[:, :, 2]
    live = local_segment.reshape(-1, 4)[:, 0] >= 0
    step = tok_rows // 2
    own, theirs = [], []
    for start in range(0, tok_rows, step):
        rows = slice(start, start + step)
        asking = queries[:, rows]
        if own:
            asking, own[-1] = lax.optimization_barrier((asking, own[-1]))
        context = attend_pairs(asking, keys, vectors, local_segment[rows], local_segment)
        attn_out = jnp.einsum("ptn,pdn->td", context, go, preferred_element_type=jnp.float32)
        hidden = tokens[rows].astype(jnp.float32) + attn_out
        normal = layer_norm(hidden.reshape(step // 4, -1), merge_gain)
        merged = jnp.where(live[start // 4 : (start + step) // 4, None], normal, 0.0)
        own.append(merged.astype(jnp.bfloat16))
        theirs.append(lax.ppermute(own[-1], "inner", [(0, 1), (1, 0)]))
    n_dp = lax.axis_size("dp")
    half_rows = tok_rows // 4
    slots = 4 * half_rows // n_dp
    owner_col = owners[:, 0]
    chosen = (owner_col[:, None] == jnp.arange(n_dp, dtype=jnp.int32)[None, :]).astype(jnp.int32)
    earlier = jnp.cumsum(chosen, axis=0) - chosen
    rank = jnp.sum(earlier * chosen, axis=1)
    target = owner_col * slots + rank
    target = jnp.where(
        lax.axis_index("inner") == 0,
        target,
        jnp.concatenate([target[half_rows:], target[:half_rows]]),
    )
    place = (jnp.arange(n_dp * slots, dtype=jnp.int32)[:, None] == target[None, :]).astype(jnp.bfloat16)
    first = merge_and_route(own + theirs, merge_halves[0], place, 1)
    place, _ = lax.optimization_barrier((place, first))
    second = merge_and_route(own + theirs, merge_halves[1], place, 2)
    return jnp.concatenate([first, second], axis=1)


def solution(mesh):
    placed = (
        P(("dp", "inner"), None),
        P(),
        P(None, "dp", "inner"),
        P("inner", "dp"),
        P(),
        P("dp", "inner"),
        P("dp"),
        P("dp", None),
    )
    ringed = dict(mesh.shape) == {"dp": 16, "inner": 2}
    return jax.shard_map(
        local_ring if ringed else local, mesh=mesh, in_specs=placed, out_specs=P("dp", "inner"), check_vma=False
    )
```

```python
import functools

import jax
import jax.numpy as jnp
from jax import lax
from jax.experimental import pallas as pl
from jax.experimental.pallas import tpu as pltpu
from jax.sharding import PartitionSpec as P

MESH = pl.DeviceIdType.MESH

HEAD_DIM = 104


EPS = 1e-06
NEG = -1e30


def layer_norm(values, gain):
    values = values.astype(jnp.float32)
    center = values - jnp.mean(values, axis=-1, keepdims=True)
    spread = jnp.mean(center * center, axis=-1, keepdims=True)
    return center * lax.rsqrt(spread + EPS) * gain


def attend_block(queries, keys, vectors, segment):
    scale = queries.shape[-1] ** (-0.5)
    scores = jnp.einsum("qhe,khe->hqk", queries, keys, preferred_element_type=jnp.float32) * scale
    visible = segment[:, None] == segment[None, :]
    scores = jnp.where(visible[None, :, :], scores, NEG)
    top = jnp.max(scores, axis=-1, keepdims=True)
    weights = jnp.exp(scores - top)
    probs = (weights / jnp.sum(weights, axis=-1, keepdims=True)).astype(jnp.bfloat16)
    context = jnp.einsum("hqk,khe->qhe", probs, vectors, preferred_element_type=jnp.float32)
    return context.astype(jnp.bfloat16)


def split_heads(projected):
    shaped = projected.reshape(3, projected.shape[1], projected.shape[2] // HEAD_DIM, HEAD_DIM)
    return (shaped[0], shaped[1], shaped[2])


def local(tokens, attn_gain, qkv_weight, out_weight, merge_gain, merge_weight, segment_ids, owners):
    tok_rows = tokens.shape[0]
    local_segment = lax.dynamic_slice_in_dim(
        segment_ids, lax.axis_index("inner") * tok_rows, tok_rows
    )
    normed = layer_norm(tokens, attn_gain).astype(jnp.bfloat16)
    qkv_part = lax.all_gather(qkv_weight, "inner", axis=2, tiled=True)
    projected = jnp.einsum(
        "td,cdh->cth",
        normed,
        lax.all_gather(qkv_part, "dp", axis=1, tiled=True),
        preferred_element_type=jnp.float32,
    )
    queries, keys, vectors = split_heads(projected.astype(jnp.bfloat16))
    context = attend_block(queries, keys, vectors, local_segment).reshape(tok_rows, -1)
    out_part = lax.all_gather(out_weight, "inner", axis=0, tiled=True)
    attn_out = jnp.dot(
        context,
        lax.all_gather(out_part, "dp", axis=1, tiled=True),
        preferred_element_type=jnp.float32,
    )
    hidden = tokens.astype(jnp.float32) + attn_out
    quad_rows = hidden.reshape(tok_rows // 4, -1)
    live = local_segment.reshape(-1, 4)[:, 0] >= 0
    merged = jnp.where(live[:, None], layer_norm(quad_rows, merge_gain), 0.0).astype(jnp.bfloat16)
    merge_full = lax.all_gather(merge_weight, "dp", axis=0, tiled=True)
    features = jnp.dot(
        lax.all_gather(merged, "inner", axis=0, tiled=True),
        merge_full,
        preferred_element_type=jnp.float32,
    ).astype(jnp.bfloat16)
    n_dp = lax.axis_size("dp")
    group_rows = features.shape[0]
    slots = 2 * group_rows // n_dp
    owner_col = owners[:, 0]
    chosen = (owner_col[:, None] == jnp.arange(n_dp, dtype=jnp.int32)[None, :]).astype(jnp.int32)
    earlier = jnp.cumsum(chosen, axis=0) - chosen
    rank = jnp.sum(earlier * chosen, axis=1)
    target = owner_col * slots + rank
    source_row = (
        jnp.full((n_dp * slots,), group_rows, jnp.int32)
        .at[target]
        .set(jnp.arange(group_rows, dtype=jnp.int32))
    )
    padded = jnp.concatenate([features, jnp.zeros((1, features.shape[1]), jnp.bfloat16)], axis=0)
    outgoing = padded[source_row]
    return lax.all_to_all(outgoing, "dp", split_axis=0, concat_axis=0, tiled=True)


RING = 8


def chip_of(place):
    place = lax.rem(place + 2 * RING, RING)
    row = place // 4
    return 2 * (place + row * (7 - 2 * place)) + row


def gather_kernel(sq, so, gq, go, local_sem, send_sem, recv_sem):
    x = lax.axis_index("inner")
    dp = lax.axis_index("dp")
    core = lax.rem(dp, 2)
    chip = dp // 2
    z, y = chip // 2, lax.rem(chip, 2)
    place = z + y * (7 - 2 * z)
    right = (chip_of(place + 1) * 2 + core, x)
    left = (chip_of(place - 1) * 2 + core, x)
    across = (dp, 1 - x)
    sibling = (chip * 2 + 1 - core, x)
    mine = 2 * x + core
    far = 2 * (1 - x) + core
    split = 112

    barrier = pltpu.get_barrier_semaphore()
    for other in (right, left, across, sibling):
        pl.semaphore_signal(barrier, inc=1, device_id=other, device_id_type=MESH)
    pl.semaphore_wait(barrier, 4)

    pairs = ((sq, gq), (so, go))
    kept = []
    for a, (shard, whole) in enumerate(pairs):
        copy = pltpu.make_async_copy(shard, whole.at[mine, chip], local_sem.at[a])
        copy.start()
        kept.append(copy)

    sent = []

    def block(whole, plane, dist, rows):
        ref = whole.at[plane, chip_of(place + dist)]
        return ref if rows is None else ref.at[pl.ds(*rows)]

    def send(a, slot, plane, dist, device, rows=None):
        whole = pairs[a][1]
        target = block(whole, plane, dist, rows)
        source = pairs[a][0] if plane is mine and dist == 0 else target
        if plane is mine and dist == 0 and rows is not None:
            source = source.at[pl.ds(*rows)]
        copy = pltpu.make_async_remote_copy(
            src_ref=source,
            dst_ref=target,
            send_sem=send_sem.at[a, slot],
            recv_sem=recv_sem.at[a, slot],
            device_id=device,
            device_id_type=MESH,
        )
        copy.start()
        sent.append(copy)

    def arrived(a, slot, plane, dist, device, rows=None):
        target = block(pairs[a][1], plane, dist, rows)
        pltpu.make_async_remote_copy(
            src_ref=target,
            dst_ref=target,
            send_sem=send_sem.at[a, slot],
            recv_sem=recv_sem.at[a, slot],
            device_id=device,
            device_id_type=MESH,
        ).wait_recv()

    def spread(a, plane, dist):
        index = dist % RING
        if a == 0:
            send(a, 8 + index, plane, dist, across)
        send(a, (16 if plane is mine else 24) + index, plane, dist, sibling)

    top, bottom = (0, split), (split, sq.shape[0] - split)
    rings = ((0, mine, 0), (1, mine, 0), (1, far, 32))
    send(1, 8, mine, 0, across)
    for a, plane, base in rings:
        if plane is far:
            arrived(1, 8, far, 0, across)
        send(a, base, plane, 0, right)
        send(a, base + 4, plane, 0, left)
        spread(a, plane, 0)
    for step in range(1, 4):
        for a, plane, base in rings:
            arrived(a, base + step - 1, plane, -step, left)
            send(a, base + step, plane, -step, right, top if step == 3 else None)
            spread(a, plane, -step)
            arrived(a, base + 4 + step - 1, plane, step, right)
            send(a, base + 4 + step, plane, step, left, bottom if step == 3 else None)
            spread(a, plane, step)
    for a, plane, base in rings:
        arrived(a, base + 3, plane, 4, left, top)
        arrived(a, base + 7, plane, 4, right, bottom)
        spread(a, plane, 4)
    order = (0, -1, 1, -2, 2, -3, 3, 4)
    for dist in order:
        arrived(0, 8 + dist % RING, far, dist, across)
        send(0, 24 + dist % RING, far, dist, sibling)
    near_other = 2 * x + 1 - core
    far_other = 2 * (1 - x) + 1 - core
    for dist in order:
        for a in range(2):
            arrived(a, 16 + dist % RING, near_other, dist, sibling)
            arrived(a, 24 + dist % RING, far_other, dist, sibling)
    for copy in sent:
        copy.wait_send()
    for copy in kept:
        copy.wait()


def gather_heads(sq, so):
    return pl.pallas_call(
        gather_kernel,
        out_shape=(
            jax.ShapeDtypeStruct((4, RING) + sq.shape, sq.dtype),
            jax.ShapeDtypeStruct((4, RING) + so.shape, so.dtype),
        ),
        in_specs=[pl.BlockSpec(memory_space=pl.ANY)] * 2,
        out_specs=(pl.BlockSpec(memory_space=pl.ANY),) * 2,
        scratch_shapes=[
            pltpu.SemaphoreType.DMA((2,)),
            pltpu.SemaphoreType.DMA((2, 40)),
            pltpu.SemaphoreType.DMA((2, 40)),
        ],
        compiler_params=pltpu.CompilerParams(collective_id=0, has_side_effects=True),
        cost_estimate=pl.CostEstimate(flops=0, bytes_accessed=200_000_000, transcendentals=0),
    )(sq, so)


TAIL_COLS = 256


def tail_kernel(parts, *refs):
    merge_parts(refs[:parts], *refs[parts:])


def merge_parts(pieces, weight, place, out, rows, wide, feat, load_sem, keep_sem, send_sem, recv_sem):
    x = lax.axis_index("inner")
    me = lax.axis_index("dp")
    peers = lax.axis_size("dp")
    piece = pieces[0].shape[0]
    slots = out.shape[0] // peers
    chunks = weight.shape[1] // TAIL_COLS

    loads = [
        pltpu.make_async_copy(ref, rows.at[pl.ds(number * piece, piece)], load_sem.at[chunks + number])
        for number, ref in enumerate(pieces)
    ]
    for chunk in range(chunks):
        loads.append(
            pltpu.make_async_copy(
                weight.at[:, pl.ds(chunk * TAIL_COLS, TAIL_COLS)], wide.at[chunk], load_sem.at[chunk]
            )
        )
    for load in loads:
        load.start()

    barrier = pltpu.get_barrier_semaphore()
    for step in range(1, peers):
        other = lax.rem(me + step, peers)
        pl.semaphore_signal(barrier, inc=1, device_id=(other, x), device_id_type=MESH)
    for number in range(len(pieces)):
        loads[number].wait()

    copies = []
    for chunk in range(chunks):
        loads[len(pieces) + chunk].wait()
        product = jnp.dot(rows[...], wide[chunk], preferred_element_type=jnp.float32)
        feat[chunk] = jnp.dot(
            place[...], product.astype(jnp.bfloat16), preferred_element_type=jnp.float32
        ).astype(jnp.bfloat16)
        if chunk == 0:
            pl.semaphore_wait(barrier, peers - 1)
        columns = pl.ds(chunk * TAIL_COLS, TAIL_COLS)
        landing = out.at[pl.ds(pl.multiple_of(me * slots, slots), slots), columns]
        for step in range(1, peers):
            other = lax.rem(me + step, peers)
            copy = pltpu.make_async_remote_copy(
                src_ref=feat.at[chunk, pl.ds(pl.multiple_of(other * slots, slots), slots)],
                dst_ref=landing,
                send_sem=send_sem.at[chunk, step],
                recv_sem=recv_sem.at[chunk, step],
                device_id=(other, x),
                device_id_type=MESH,
            )
            copy.start()
            copies.append(copy)
        keep = pltpu.make_async_copy(
            feat.at[chunk, pl.ds(pl.multiple_of(me * slots, slots), slots)], landing, keep_sem.at[chunk]
        )
        keep.start()
        copies.append(keep)
    for chunk in range(chunks):
        columns = pl.ds(chunk * TAIL_COLS, TAIL_COLS)
        for step in range(1, peers):
            giver = lax.rem(me + peers - step, peers)
            landing = out.at[pl.ds(pl.multiple_of(giver * slots, slots), slots), columns]
            pltpu.make_async_remote_copy(
                src_ref=landing,
                dst_ref=landing,
                send_sem=send_sem.at[chunk, step],
                recv_sem=recv_sem.at[chunk, step],
                device_id=(giver, x),
                device_id_type=MESH,
            ).wait_recv()
    for number, copy in enumerate(copies):
        if number % peers == peers - 1:
            copy.wait()
        else:
            copy.wait_send()


def merge_and_route(pieces, weight, place):
    peers = lax.axis_size("dp")
    out_rows, group = place.shape
    depth, columns = weight.shape
    chunks = columns // TAIL_COLS
    return pl.pallas_call(
        functools.partial(tail_kernel, len(pieces)),
        out_shape=jax.ShapeDtypeStruct((out_rows, columns), jnp.bfloat16),
        in_specs=[pl.BlockSpec(memory_space=pltpu.VMEM)] * len(pieces)
        + [pl.BlockSpec(memory_space=pl.ANY), pl.BlockSpec(memory_space=pltpu.VMEM)],
        out_specs=pl.BlockSpec(memory_space=pltpu.VMEM),
        scratch_shapes=[
            pltpu.VMEM((group, depth), jnp.bfloat16),
            pltpu.VMEM((chunks, depth, TAIL_COLS), jnp.bfloat16),
            pltpu.VMEM((chunks, out_rows, TAIL_COLS), jnp.bfloat16),
            pltpu.SemaphoreType.DMA((chunks + len(pieces),)),
            pltpu.SemaphoreType.DMA((chunks,)),
            pltpu.SemaphoreType.DMA((chunks, peers)),
            pltpu.SemaphoreType.DMA((chunks, peers)),
        ],
        compiler_params=pltpu.CompilerParams(
            collective_id=1, has_side_effects=True, vmem_limit_bytes=56 * 1024 * 1024
        ),
        cost_estimate=pl.CostEstimate(
            flops=2 * group * depth * columns, bytes_accessed=2 * depth * columns, transcendentals=0
        ),
    )(*pieces, weight, place)


def pair_shards(qkv_weight, out_weight):
    depth = qkv_weight.shape[1]
    half = qkv_weight.shape[2] // 2
    core = lax.rem(lax.axis_index("dp"), 2)
    heads = qkv_weight.reshape(3, depth, 2, half).transpose(2, 1, 0, 3).reshape(2, depth, 3 * half)
    outs = out_weight.reshape(2, half, depth).transpose(0, 2, 1)
    both = jnp.concatenate([heads, outs], axis=2)
    keep = jnp.where(core == 0, both[0], both[1])
    give = jnp.where(core == 0, both[1], both[0])
    n_dp = lax.axis_size("dp")
    got = lax.ppermute(give, "dp", [(i, i ^ 1) for i in range(n_dp)])
    shard = jnp.concatenate(
        [jnp.where(core == 0, keep, got), jnp.where(core == 0, got, keep)], axis=0
    )
    return shard[:, : 3 * half], shard[:, 3 * half :]


def attend_pairs(queries, keys, vectors, own_segment, segment):
    pairs, rows = queries.shape[:2]
    scale = HEAD_DIM ** (-0.5)
    scores = jnp.einsum("pqhe,pkhe->phqk", queries, keys, preferred_element_type=jnp.float32) * scale
    visible = own_segment[:, None] == segment[None, :]
    scores = jnp.where(visible[None, None], scores, NEG)
    top = jnp.max(scores, axis=-1, keepdims=True)
    weights = jnp.exp(scores - top)
    probs = (weights / jnp.sum(weights, axis=-1, keepdims=True)).astype(jnp.bfloat16)
    context = jnp.einsum("phqk,pkhe->pqhe", probs, vectors, preferred_element_type=jnp.float32)
    return context.astype(jnp.bfloat16).reshape(pairs, rows, 2 * HEAD_DIM)


def local_ring(tokens, attn_gain, qkv_weight, out_weight, merge_gain, merge_weight, segment_ids, owners):
    tok_rows, width = tokens.shape
    local_segment = lax.dynamic_slice_in_dim(
        segment_ids, lax.axis_index("inner") * tok_rows, tok_rows
    )
    merge_full = lax.all_gather(merge_weight, "dp", axis=0, tiled=True)
    sq, so = pair_shards(qkv_weight, out_weight)
    gq, go = gather_heads(sq, so)
    gq = gq.reshape(4, width, sq.shape[1])
    go = go.reshape(4, width, so.shape[1])
    normed = layer_norm(tokens, attn_gain).astype(jnp.bfloat16)
    projected = jnp.einsum("td,pdn->ptn", normed, gq, preferred_element_type=jnp.float32)
    shaped = projected.astype(jnp.bfloat16).reshape(4, tok_rows, 3, 2, HEAD_DIM)
    queries, keys, vectors = shaped[:, :, 0], shaped[:, :, 1], shaped[:, :, 2]
    live = local_segment.reshape(-1, 4)[:, 0] >= 0
    step = tok_rows // 2
    own, theirs = [], []
    for start in range(0, tok_rows, step):
        rows = slice(start, start + step)
        asking = queries[:, rows]
        if own:
            asking, own[-1] = lax.optimization_barrier((asking, own[-1]))
        context = attend_pairs(asking, keys, vectors, local_segment[rows], local_segment)
        attn_out = jnp.einsum("ptn,pdn->td", context, go, preferred_element_type=jnp.float32)
        hidden = tokens[rows].astype(jnp.float32) + attn_out
        normal = layer_norm(hidden.reshape(step // 4, -1), merge_gain)
        merged = jnp.where(live[start // 4 : (start + step) // 4, None], normal, 0.0)
        own.append(merged.astype(jnp.bfloat16))
        theirs.append(lax.ppermute(own[-1], "inner", [(0, 1), (1, 0)]))
    n_dp = lax.axis_size("dp")
    half_rows = tok_rows // 4
    slots = 4 * half_rows // n_dp
    owner_col = owners[:, 0]
    chosen = (owner_col[:, None] == jnp.arange(n_dp, dtype=jnp.int32)[None, :]).astype(jnp.int32)
    earlier = jnp.cumsum(chosen, axis=0) - chosen
    rank = jnp.sum(earlier * chosen, axis=1)
    target = owner_col * slots + rank
    target = jnp.where(
        lax.axis_index("inner") == 0,
        target,
        jnp.concatenate([target[half_rows:], target[:half_rows]]),
    )
    place = (jnp.arange(n_dp * slots, dtype=jnp.int32)[:, None] == target[None, :]).astype(jnp.bfloat16)
    return merge_and_route(own + theirs, merge_full, place)


def solution(mesh):
    placed = (
        P(("dp", "inner"), None),
        P(),
        P(None, "dp", "inner"),
        P("inner", "dp"),
        P(),
        P("dp", "inner"),
        P("dp"),
        P("dp", None),
    )
    ringed = dict(mesh.shape) == {"dp": 16, "inner": 2}
    return jax.shard_map(
        local_ring if ringed else local, mesh=mesh, in_specs=placed, out_specs=P("dp", "inner"), check_vma=False
    )
```
